512 devices in a mesh: ctx: 64 (over x, z), tp: 8 (over y, core).
Axes of the slice: x: 4, y: 4, z: 16, core: 2. Of those that a mesh axis runs over, the one named last changes fastest.
Arguments:
- gate_in: bfloat16 [8192, 4096], P('ctx', 'tp'), may hold values from -6 to 6
- value_in: bfloat16 [8192, 4096], P('ctx', 'tp'), may hold values from -6 to 6
- gate_out: bfloat16 [8192, 4096], P('ctx', 'tp'), may hold values from -6 to 6
- filters: bfloat16 [8192, 4096], P('ctx', 'tp'), may hold values from -1.1 to 1.1, as said below
- skip_gain: float32 [4096], P('tp'), may hold values from -4 to 4
- out_weight: bfloat16 [4096, 4096], P('ctx', 'tp'), may hold values from -0.09375 to 0.09375
Outputs:
- mixed: bfloat16 [8192, 4096], P('ctx', 'tp')
The draws below stay inside these ranges and needn't reach their ends.
Inputs may be any that keep to these rules, and one draw needn't show every extreme that they name: `filters`: one filter a channel over 8192 lags.
All inputs are finite; a program needn't handle non-finite values.
Results may differ from the reference program's by a relative error of at most 0.013.
Values may be sent and summed in bfloat16 or wider, within the bound.
No kernel may reach another device: no remote copies, remote signals or barrier semaphores. Data moves between devices by JAX's collectives and lax.ppermute only.
A program may use at most 64 MiB of HBM per device.

```python
import jax
import jax.numpy as jnp
from jax import lax

CH = 4096
DW = 4096
SEQ = 8192


def draw_filters(key, part):
    key = jax.random.fold_in(key, 7)
    key_noise, key_slow, key_rate, key_len, key_tail, key_trate = jax.random.split(key, 6)
    lags = jnp.arange(SEQ, dtype=jnp.float32)[:, None]
    slow_mask = jax.random.bernoulli(key_slow, 0.5, (1, CH))
    slow_rate = jax.random.uniform(key_rate, (1, CH), jnp.float32, 0.3, 2.0) / SEQ
    fast_len = jax.random.uniform(key_len, (1, CH), jnp.float32, 30.0, 50.0)
    rate = jnp.where(slow_mask, slow_rate, 1.0 / fast_len)
    amplitude = jnp.sqrt(2.0 * rate)
    tail_rate = jax.random.uniform(key_trate, (1, CH), jnp.float32, 0.1, 0.6) / SEQ
    tail_scale = 0.5 * float(SEQ) ** (-0.5)
    noise = jax.random.truncated_normal(key_noise, -4.0, 4.0, (SEQ, CH), jnp.float32)
    tail_noise = jax.random.truncated_normal(key_tail, -3.0, 3.0, (SEQ, CH), jnp.float32)
    head = amplitude * jnp.exp(-rate * lags) * noise
    tail = tail_scale * jnp.exp(-tail_rate * lags) * tail_noise
    values = head + tail
    return values.astype(jnp.bfloat16)


def levels(own_key, extent, pieces, low, largest):
    def one(dim, parts):
        draws = jax.random.uniform(jax.random.fold_in(jax.random.fold_in(own_key, 6), dim), (parts,), jnp.float32, low / len(pieces), largest / len(pieces))
        return jnp.repeat(jnp.exp(draws), extent[dim] // parts).reshape((-1,) + (1,) * (len(extent) - dim - 1))

    factor_of = one(*pieces[0])
    for cut in pieces[1:]:
        factor_of = factor_of * one(*cut)
    return factor_of


def scatter_about(rng, shape, scale, limit, pieces=(), kind=jnp.bfloat16):
    loudness = levels(rng, shape, pieces, -0.22, 0.18) if pieces else 1.0
    array = jax.random.normal(rng, shape, jnp.float32) * scale * loudness
    return jnp.minimum(jnp.maximum(array, -limit), limit).astype(kind)


def setup_inputs(seed: int = 0) -> dict:
    key_list = jax.random.split(jax.random.key(seed), 7)
    gate_in = scatter_about(key_list[0], (SEQ, CH), 1.0, 6.0, ((0, 64), (1, 8)))
    value_in = scatter_about(key_list[1], (SEQ, CH), 1.0, 6.0, ((0, 64), (1, 8)))
    gate_out = scatter_about(key_list[2], (SEQ, CH), 1.0, 6.0, ((0, 64), (1, 8)))
    filters = draw_filters(jax.random.fold_in(key_list[6], 71), 0)
    skip_gain = scatter_about(key_list[4], (CH,), 1.0, 4.0, ((0, 8),), jnp.float32)
    out_weight = scatter_about(key_list[5], (CH, DW), CH ** -0.5, 0.09375, ((0, 64), (1, 8)))
    return {"gate_in": gate_in, "value_in": value_in, "gate_out": gate_out, "filters": filters, "skip_gain": skip_gain, "out_weight": out_weight}


def causal_conv(signal_f, filter_f):
    length = 2 * SEQ
    spec = jnp.fft.rfft(signal_f, n=length, axis=0) * jnp.fft.rfft(filter_f, n=length, axis=0)
    return jnp.fft.irfft(spec, n=length, axis=0)[:SEQ]


def reference(gate_in, value_in, gate_out, filters, skip_gain, out_weight):
    signal = (gate_in.astype(jnp.float32) * value_in.astype(jnp.float32)).astype(jnp.bfloat16)
    signal_f = signal.astype(jnp.float32)
    filter_f = filters.astype(jnp.float32)
    group_width = 256 if CH % 256 == 0 else CH
    groups = CH // group_width
    sig_groups = jnp.transpose(signal_f.reshape(SEQ, groups, group_width), (1, 0, 2))
    fil_groups = jnp.transpose(filter_f.reshape(SEQ, groups, group_width), (1, 0, 2))
    conv_groups = lax.map(lambda pair: causal_conv(pair[0], pair[1]), (sig_groups, fil_groups))
    conv = jnp.transpose(conv_groups, (1, 0, 2)).reshape(SEQ, CH).astype(jnp.bfloat16)
    gated = (gate_out.astype(jnp.float32) * (conv.astype(jnp.float32) + skip_gain[None, :] * signal_f)).astype(jnp.bfloat16)
    return jnp.dot(gated, out_weight, preferred_element_type=jnp.float32).astype(jnp.bfloat16)
```

```python
import math

import jax
import jax.numpy as jnp
import numpy as np
from jax import lax
from jax.experimental import pallas as pl
from jax.experimental.pallas import tpu as pltpu
from jax.sharding import Mesh
from jax.sharding import PartitionSpec as P

F32 = jnp.float32
BF16 = jnp.bfloat16
SEQ = 8192
BLOCK = 128
NBLK = SEQ // BLOCK
VMEM_LIMIT = 40 * 1024 * 1024


def split_table(values):
    values = np.asarray(values, np.float64)
    high = values.astype(np.float32).astype(BF16)
    low = (values - high.astype(np.float64)).astype(np.float32).astype(BF16)
    return high, low


def tables():
    n1 = np.arange(NBLK)
    k1 = np.arange(NBLK) + 0.25
    n2 = np.arange(BLOCK)
    ang = 2.0 * math.pi / NBLK * (k1[:, None] * n1[None, :])
    first = np.concatenate([np.cos(ang), -np.sin(ang)], 0)
    first = np.concatenate(split_table(first), 1)
    tw = 2.0 * math.pi / SEQ * (k1[:, None] * n2[None, :])
    twist = np.stack([np.cos(tw), -np.sin(tw)]).astype(np.float32)
    th = 2.0 * math.pi / BLOCK * ((n2[:, None] * n2[None, :]) % BLOCK)
    c, s = np.cos(th), np.sin(th)
    fwd = np.block([[c, -s], [s, c]])
    second = np.stack(split_table(fwd) + split_table(fwd.T))
    last = np.concatenate([np.cos(ang.T), -np.sin(ang.T)], 1) / SEQ
    high, low = split_table(last)
    last = np.concatenate([high, high, low], 1)
    return first, twist, second, last


def split(x):
    high = x.astype(BF16)
    return high, (x - high.astype(F32)).astype(BF16)


def mm(a, b):
    return jnp.dot(a, b, preferred_element_type=F32)


def pack_kernel(gi_ref, vi_ref, f_ref, out_ref):
    signal = (gi_ref[...].astype(F32) * vi_ref[...].astype(F32)).astype(BF16)
    sig_t = signal.astype(F32).T.reshape(NBLK, 8, BLOCK)
    fil_t = f_ref[...].astype(F32).T.reshape(NBLK, 8, BLOCK)
    out_ref[...] = jnp.concatenate([sig_t, fil_t], 1).astype(BF16)


def conv_kernel(r_ref, first_ref, twist_ref, second_ref, last_ref, out_ref, xs, xx, hi, lo, spec, dd, ys):
    xs[...] = r_ref[...].astype(F32)
    for c in range(8):
        for part in range(2):
            x = xs[:, 8 * part + c, :].astype(BF16)
            at = pl.ds((2 * c + part) * BLOCK, BLOCK)
            xx[0:NBLK, at] = x
            xx[NBLK:, at] = x
    tre, tim = twist_ref[0], twist_ref[1]
    for j in range(16):
        a = mm(first_ref[...], xx[:, j * BLOCK : (j + 1) * BLOCK])
        re, im = a[:NBLK], a[NBLK:]
        turned = jnp.concatenate([re * tre - im * tim, re * tim + im * tre], 1)
        rows = pl.ds(j * NBLK, NBLK)
        hi[rows, :], lo[rows, :] = split(turned)
    spec[...] = mm(hi[...], second_ref[0]) + mm(lo[...], second_ref[0]) + mm(hi[...], second_ref[1])
    for c in range(8):
        s = spec[pl.ds(2 * c * NBLK, NBLK), :]
        f = spec[pl.ds((2 * c + 1) * NBLK, NBLK), :]
        sr, si, fr, fi = s[:, :BLOCK], s[:, BLOCK:], f[:, :BLOCK], f[:, BLOCK:]
        rows = pl.ds(c * NBLK, NBLK)
        hi[rows, :], lo[rows, :] = split(jnp.concatenate([sr * fr - si * fi, sr * fi + si * fr], 1))
    half = pl.ds(0, 8 * NBLK)
    spec[half, :] = (
        mm(hi[half, :], second_ref[2]) + mm(lo[half, :], second_ref[2]) + mm(hi[half, :], second_ref[3])
    )
    for c in range(8):
        b = spec[pl.ds(c * NBLK, NBLK), :]
        br, bi = b[:, :BLOCK], b[:, BLOCK:]
        d_hi, d_lo = split(jnp.concatenate([br * tre + bi * tim, bi * tre - br * tim], 0))
        at = pl.ds(c * BLOCK, BLOCK)
        dd[0:128, at] = d_hi
        dd[128:256, at] = d_lo
        dd[256:384, at] = d_hi
    y = mm(last_ref[...], dd[...])
    for c in range(8):
        ys[:, c, :] = y[:, c * BLOCK : (c + 1) * BLOCK]
    out_ref[...] = ys[...].astype(BF16)


def gate_kernel(r_ref, gi_ref, vi_ref, go_ref, skip_ref, out_ref):
    conv = r_ref[...].astype(F32).reshape(8 * NBLK, BLOCK).T
    signal = (gi_ref[...].astype(F32) * vi_ref[...].astype(F32)).astype(BF16).astype(F32)
    out_ref[...] = (go_ref[...].astype(F32) * (conv + skip_ref[...] * signal)).astype(BF16)


def project_kernel(core_ref, g_ref, w_ref, out_ref):
    total = jnp.zeros(out_ref.shape, F32)
    for y in range(4):
        total += mm(g_ref[y], w_ref[:, y].reshape(512, 512))
    out_ref[...] = total


def project_end_kernel(core_ref, g_ref, w_ref, p_ref, out_ref):
    total = p_ref[...]
    for y in range(4):
        total += mm(g_ref[y], w_ref[:, y].reshape(512, 512))
    out_ref[...] = total.astype(BF16)


PARAMS = pltpu.CompilerParams(vmem_limit_bytes=VMEM_LIMIT)


def shape(dims, kind=BF16):
    return jax.ShapeDtypeStruct(dims, kind)


def project(core, gathered, weight, partial=None):
    ins = [
        pl.BlockSpec((4, BLOCK, 512), lambda i, c: (0, 0, 0)),
        pl.BlockSpec((8, 4, 64, 512), lambda i, c: (c[0], 0, 0, 0)),
    ]
    args = [gathered, weight]
    body, kind = project_kernel, F32
    if partial is not None:
        ins.append(pl.BlockSpec((BLOCK, 512), lambda i, c: (0, 0)))
        args.append(partial)
        body, kind = project_end_kernel, BF16
    return pl.pallas_call(
        body,
        grid_spec=pltpu.PrefetchScalarGridSpec(
            num_scalar_prefetch=1,
            grid=(1,),
            in_specs=ins,
            out_specs=pl.BlockSpec((BLOCK, 512), lambda i, c: (0, 0)),
        ),
        out_shape=shape((BLOCK, 512), kind),
        compiler_params=PARAMS,
    )(core, *args)


def per_device(gate_in, value_in, gate_out, filters, skip_gain, out_weight):
    first, twist, second, last = tables()
    packed = pl.pallas_call(
        pack_kernel, out_shape=shape((NBLK, 16, BLOCK)), compiler_params=PARAMS
    )(gate_in, value_in, filters)
    near = lax.all_gather(out_weight, "x", axis=0)
    packed, near = lax.optimization_barrier((packed, near))
    weight = lax.all_gather(near, "z", axis=0)
    moved = lax.all_to_all(packed, ("x", "z"), split_axis=0, concat_axis=0, tiled=True)
    conv = pl.pallas_call(
        conv_kernel,
        out_shape=shape((NBLK, 8, BLOCK)),
        scratch_shapes=[
            pltpu.VMEM((NBLK, 16, BLOCK), F32),
            pltpu.VMEM((128, 16 * BLOCK), BF16),
            pltpu.VMEM((16 * NBLK, 256), BF16),
            pltpu.VMEM((16 * NBLK, 256), BF16),
            pltpu.VMEM((16 * NBLK, 256), F32),
            pltpu.VMEM((384, 8 * BLOCK), BF16),
            pltpu.VMEM((NBLK, 8, BLOCK), F32),
        ],
        compiler_params=PARAMS,
    )(moved, first, twist, second, last)
    back = lax.all_to_all(conv, ("x", "z"), split_axis=0, concat_axis=0, tiled=True)
    gated = pl.pallas_call(
        gate_kernel, out_shape=shape((BLOCK, 512)), compiler_params=PARAMS
    )(back, gate_in, value_in, gate_out, skip_gain[None, :])
    mine = lax.all_gather(gated, "y", axis=0)
    other = lax.ppermute(mine, "core", [(0, 1), (1, 0)])
    core = lax.axis_index("core").astype(jnp.int32)[None]
    partial = project(core, mine, weight)
    return project(1 - core, other, weight, partial)


def solution(mesh):
    fine = Mesh(mesh.devices.reshape(4, 16, 4, 2), ("x", "z", "y", "core"))
    rows, cols = ("x", "z"), ("y", "core")
    whole = P(rows, cols)
    return jax.shard_map(
        per_device,
        mesh=fine,
        in_specs=(whole, whole, whole, whole, P(cols), whole),
        out_specs=whole,
        check_vma=False,
    )
```

```python
import math

import jax
import jax.numpy as jnp
import numpy as np
from jax import lax
from jax.experimental import pallas as pl
from jax.experimental.pallas import tpu as pltpu
from jax.sharding import Mesh
from jax.sharding import PartitionSpec as P

F32 = jnp.float32
BF16 = jnp.bfloat16
SEQ = 8192
BLOCK = 128
NBLK = SEQ // BLOCK
VMEM_LIMIT = 60 * 1024 * 1024


def tables():
    n1 = np.arange(NBLK)
    k1 = np.arange(NBLK) + 0.25
    n2 = np.arange(BLOCK)
    ang = 2.0 * math.pi / NBLK * (k1[:, None] * n1[None, :])
    first = np.concatenate([np.cos(ang), -np.sin(ang)], 0)
    first = np.concatenate([first, first], 1).astype(np.float32)
    tw = 2.0 * math.pi / SEQ * (k1[:, None] * n2[None, :])
    twist = np.stack([np.cos(tw), -np.sin(tw)]).astype(np.float32)
    th = 2.0 * math.pi / BLOCK * ((n2[:, None] * n2[None, :]) % BLOCK)
    c, s = np.cos(th), np.sin(th)
    fwd = np.block([[c, -s], [s, c]])
    second = np.stack([fwd, fwd.T]).astype(np.float32)
    last = (np.concatenate([np.cos(ang.T), -np.sin(ang.T)], 1) / SEQ).astype(np.float32)
    return first, twist, second, last


def split(x):
    high = x.astype(BF16)
    return high, (x - high.astype(F32)).astype(BF16)


def mm(a, b):
    return jnp.dot(a, b, preferred_element_type=F32)


def fetch(sources, buffers, sems):
    copies = [pltpu.make_async_copy(s, b, sems.at[i]) for i, (s, b) in enumerate(zip(sources, buffers))]
    for copy in copies:
        copy.start()
    return copies


def pack_kernel(gi_hbm, vi_hbm, f_hbm, out_ref, gi_ref, vi_ref, f_ref, sems):
    for copy in fetch((gi_hbm, vi_hbm, f_hbm), (gi_ref, vi_ref, f_ref), sems):
        copy.wait()
    signal = (gi_ref[...].astype(F32) * vi_ref[...].astype(F32)).astype(BF16)
    sig_t = signal.astype(F32).T.reshape(NBLK, 8, BLOCK)
    fil_t = f_ref[...].astype(F32).T.reshape(NBLK, 8, BLOCK)
    out_ref[...] = jnp.concatenate([sig_t, fil_t], 1).astype(BF16)


def conv_kernel(
    r_ref, first_hbm, twist_hbm, second_hbm, last_hbm, out_ref,
    xs, xx, hi, lo, spec, dd, ys, first_ref, twist_ref, second_ref, last_ref, sems,
):
    copies = fetch(
        (first_hbm, twist_hbm, second_hbm, last_hbm), (first_ref, twist_ref, second_ref, last_ref), sems
    )
    xs[...] = r_ref[...].astype(F32)
    for c in range(8):
        for part in range(2):
            x = xs[:, 8 * part + c, :].astype(BF16)
            at = pl.ds((2 * c + part) * BLOCK, BLOCK)
            xx[0:NBLK, at] = x
            xx[NBLK:, at] = x
    copies[0].wait()
    copies[1].wait()
    tre, tim = twist_ref[0], twist_ref[1]
    f_hi, f_lo = split(first_ref[...])
    lanes = lax.broadcasted_iota(jnp.int32, f_hi.shape, 1)
    first = jnp.where(lanes < NBLK, f_hi.astype(F32), f_lo.astype(F32)).astype(BF16)
    for j in range(16):
        a = mm(first, xx[:, j * BLOCK : (j + 1) * BLOCK])
        re, im = a[:NBLK], a[NBLK:]
        turned = jnp.concatenate([re * tre - im * tim, re * tim + im * tre], 1)
        rows = pl.ds(j * NBLK, NBLK)
        hi[rows, :], lo[rows, :] = split(turned)
    copies[2].wait()
    copies[3].wait()
    g_hi, g_lo = split(second_ref[0])
    spec[...] = mm(hi[...], g_hi) + mm(lo[...], g_hi) + mm(hi[...], g_lo)
    for c in range(8):
        s = spec[pl.ds(2 * c * NBLK, NBLK), :]
        f = spec[pl.ds((2 * c + 1) * NBLK, NBLK), :]
        sr, si, fr, fi = s[:, :BLOCK], s[:, BLOCK:], f[:, :BLOCK], f[:, BLOCK:]
        rows = pl.ds(c * NBLK, NBLK)
        hi[rows, :], lo[rows, :] = split(jnp.concatenate([sr * fr - si * fi, sr * fi + si * fr], 1))
    half = pl.ds(0, 8 * NBLK)
    g_hi, g_lo = split(second_ref[1])
    spec[half, :] = mm(hi[half, :], g_hi) + mm(lo[half, :], g_hi) + mm(hi[half, :], g_lo)
    for c in range(8):
        b = spec[pl.ds(c * NBLK, NBLK), :]
        br, bi = b[:, :BLOCK], b[:, BLOCK:]
        d_hi, d_lo = split(jnp.concatenate([br * tre + bi * tim, bi * tre - br * tim], 0))
        at = pl.ds(c * BLOCK, BLOCK)
        dd[0:128, at] = d_hi
        dd[128:256, at] = d_lo
        dd[256:384, at] = d_hi
    l_hi, l_lo = split(last_ref[...])
    y = mm(jnp.concatenate([l_hi, l_hi, l_lo], 1), dd[...])
    for c in range(8):
        ys[:, c, :] = y[:, c * BLOCK : (c + 1) * BLOCK]
    out_ref[...] = ys[...].astype(BF16)


def gate_kernel(r_ref, gi_hbm, vi_hbm, go_hbm, skip_ref, out_ref, gi_ref, vi_ref, go_ref, sems):
    copies = fetch((gi_hbm, vi_hbm, go_hbm), (gi_ref, vi_ref, go_ref), sems)
    conv = r_ref[...].astype(F32).reshape(8 * NBLK, BLOCK).T
    for copy in copies:
        copy.wait()
    signal = (gi_ref[...].astype(F32) * vi_ref[...].astype(F32)).astype(BF16).astype(F32)
    out_ref[...] = (go_ref[...].astype(F32) * (conv + skip_ref[...] * signal)).astype(BF16)


def project_kernel(mine_hbm, other_hbm, w_hbm, out_ref, g_ref, w_ref, g_sems, w_sems):
    core = lax.axis_index("core")
    g_copies = fetch((mine_hbm, other_hbm), (g_ref.at[0], g_ref.at[1]), g_sems)
    w_copies = []
    for side in range(2):
        start = 8 * (core if side == 0 else 1 - core)
        for y in range(4):
            at = 4 * side + y
            copy = pltpu.make_async_copy(w_hbm.at[pl.ds(start, 8), y], w_ref.at[at], w_sems.at[at])
            copy.start()
            w_copies.append(copy)
    total = jnp.zeros(out_ref.shape, F32)
    for at in range(8):
        if at % 4 == 0:
            g_copies[at // 4].wait()
        w_copies[at].wait()
        total += mm(g_ref[at // 4, at % 4], w_ref[at].reshape(512, 512))
    out_ref[...] = total.astype(BF16)


PARAMS = pltpu.CompilerParams(vmem_limit_bytes=VMEM_LIMIT)


def shape(dims, kind=BF16):
    return jax.ShapeDtypeStruct(dims, kind)


ANY = pl.BlockSpec(memory_space=pl.ANY)
INSIDE = pl.BlockSpec(memory_space=pltpu.VMEM)


def call(body, out, ins, scratch):
    return pl.pallas_call(
        body, out_shape=shape(out), in_specs=ins, out_specs=INSIDE, scratch_shapes=scratch, compiler_params=PARAMS
    )


def copies(count):
    return pltpu.SemaphoreType.DMA((count,))


def run_conv(moved):
    first, twist, second, last = tables()
    return call(
        conv_kernel,
        (NBLK, 8, BLOCK),
        [INSIDE, ANY, ANY, ANY, ANY],
        [
            pltpu.VMEM((NBLK, 16, BLOCK), F32),
            pltpu.VMEM((128, 16 * BLOCK), BF16),
            pltpu.VMEM((16 * NBLK, 256), BF16),
            pltpu.VMEM((16 * NBLK, 256), BF16),
            pltpu.VMEM((16 * NBLK, 256), F32),
            pltpu.VMEM((384, 8 * BLOCK), BF16),
            pltpu.VMEM((NBLK, 8, BLOCK), F32),
            pltpu.VMEM(first.shape, F32),
            pltpu.VMEM(twist.shape, F32),
            pltpu.VMEM(second.shape, F32),
            pltpu.VMEM(last.shape, F32),
            copies(4),
        ],
    )(moved, first, twist, second, last)


def per_device(gate_in, value_in, gate_out, filters, skip_gain, out_weight):
    tile = pltpu.VMEM((BLOCK, 512), BF16)
    near = lax.all_to_all(
        jnp.broadcast_to(out_weight[None], (4, 64, 512)), "x", split_axis=0, concat_axis=0, tiled=True
    )
    near, filters = lax.optimization_barrier((near, filters))
    weight = lax.all_gather(near, "z", axis=0)
    packed = call(pack_kernel, (NBLK, 16, BLOCK), [ANY] * 3, [tile] * 3 + [copies(3)])(gate_in, value_in, filters)
    moved = lax.all_to_all(packed, ("x", "z"), split_axis=0, concat_axis=0, tiled=True)
    conv = run_conv(moved)
    back = lax.all_to_all(conv, ("x", "z"), split_axis=0, concat_axis=0, tiled=True)
    gated = call(gate_kernel, (BLOCK, 512), [INSIDE, ANY, ANY, ANY, INSIDE], [tile] * 3 + [copies(3)])(
        back, gate_in, value_in, gate_out, skip_gain[None, :]
    )
    mine = lax.all_gather(gated, "y", axis=0)
    other = lax.ppermute(mine, "core", [(0, 1), (1, 0)])
    return call(
        project_kernel,
        (BLOCK, 512),
        [ANY] * 3,
        [
            pltpu.VMEM((2, 4, BLOCK, 512), BF16),
            pltpu.VMEM((8, 8, 64, 512), BF16),
            copies(2),
            copies(8),
        ],
    )(mine, other, weight)


def solution(mesh):
    fine = Mesh(mesh.devices.reshape(4, 16, 4, 2), ("x", "z", "y", "core"))
    rows, cols = ("x", "z"), ("y", "core")
    whole = P(rows, cols)
    return jax.shard_map(
        per_device,
        mesh=fine,
        in_specs=(whole, whole, whole, whole, P(cols), whole),
        out_specs=whole,
        check_vma=False,
    )
```

```python
import math

import jax
import jax.numpy as jnp
import numpy as np
from jax import lax
from jax.experimental import pallas as pl
from jax.experimental.pallas import tpu as pltpu
from jax.sharding import Mesh
from jax.sharding import PartitionSpec as P

F32 = jnp.float32
BF16 = jnp.bfloat16
SEQ = 8192
BLOCK = 128
NBLK = SEQ // BLOCK
SPARE = 16
VMEM_LIMIT = 24 * 1024 * 1024


def tables():
    n1 = np.arange(NBLK)
    k1 = np.arange(NBLK) + 0.25
    n2 = np.arange(BLOCK)
    ang = 2.0 * math.pi / NBLK * (k1[:, None] * n1[None, :])
    first = np.concatenate([np.cos(ang), -np.sin(ang)], 0)
    first = np.concatenate([first, first], 1).astype(np.float32)
    tw = 2.0 * math.pi / SEQ * (k1[:, None] * n2[None, :])
    twist = np.stack([np.cos(tw), -np.sin(tw)]).astype(np.float32)
    th = 2.0 * math.pi / BLOCK * ((n2[:, None] * n2[None, :]) % BLOCK)
    c, s = np.cos(th), np.sin(th)
    fwd = np.block([[c, -s], [s, c]])
    second = np.stack([fwd, fwd.T]).astype(np.float32)
    last = (np.concatenate([np.cos(ang.T), -np.sin(ang.T)], 1) / SEQ).astype(np.float32)
    return first, twist, second, last


def split(x):
    high = x.astype(BF16)
    return high, (x - high.astype(F32)).astype(BF16)


def mm(a, b):
    return jnp.dot(a, b, preferred_element_type=F32)


def fetch(sources, buffers, sems):
    copies = [pltpu.make_async_copy(s, b, sems.at[i]) for i, (s, b) in enumerate(zip(sources, buffers))]
    for copy in copies:
        copy.start()
    return copies


def by_owner(x):
    x = x.reshape(8, 4, 16, BLOCK)
    return jnp.stack([x[:, owner] for owner in range(4)])


def pack_kernel(gi_hbm, vi_hbm, f_hbm, go_hbm, w_hbm, out_ref, side_ref, gi_ref, vi_ref, f_ref, go_ref, w_ref, sems):
    loads = fetch((go_hbm, w_hbm, gi_hbm, vi_hbm, f_hbm), (go_ref, w_ref, gi_ref, vi_ref, f_ref), sems)
    for load in loads:
        load.wait()
    gate = by_owner(go_ref[...].astype(F32).T).reshape(4, BLOCK, BLOCK)
    w = w_ref[...].astype(F32).reshape(4, 16, 512)
    rows = [w[:, :, q * BLOCK : (q + 1) * BLOCK] for q in range(4)]
    side_ref[...] = jnp.concatenate([gate] + rows, 1).astype(BF16)
    signal = (gi_ref[...].astype(F32) * vi_ref[...].astype(F32)).astype(BF16)
    sig_t = by_owner(signal.astype(F32).T).reshape(NBLK, 8, BLOCK)
    fil_t = by_owner(f_ref[...].astype(F32).T).reshape(NBLK, 8, BLOCK)
    out_ref[...] = jnp.concatenate([sig_t, fil_t], 1).astype(BF16)


def conv_kernel(
    r_ref, skip_ref, first_hbm, twist_hbm, second_hbm, last_hbm, out_ref,
    xs, xx, hi, lo, spec, dd, ys, first_ref, twist_ref, second_ref, last_ref, sems,
):
    copies = fetch(
        (first_hbm, twist_hbm, second_hbm, last_hbm), (first_ref, twist_ref, second_ref, last_ref), sems
    )
    xs[...] = r_ref[...].astype(F32)
    for c in range(8):
        for part in range(2):
            x = xs[:, 8 * part + c, :].astype(BF16)
            at = pl.ds((2 * c + part) * BLOCK, BLOCK)
            xx[0:NBLK, at] = x
            xx[NBLK:, at] = x
    copies[0].wait()
    copies[1].wait()
    tre, tim = twist_ref[0], twist_ref[1]
    f_hi, f_lo = split(first_ref[...])
    lanes = lax.broadcasted_iota(jnp.int32, f_hi.shape, 1)
    first = jnp.where(lanes < NBLK, f_hi.astype(F32), f_lo.astype(F32)).astype(BF16)
    for j in range(16):
        a = mm(first, xx[:, j * BLOCK : (j + 1) * BLOCK])
        re, im = a[:NBLK], a[NBLK:]
        turned = jnp.concatenate([re * tre - im * tim, re * tim + im * tre], 1)
        rows = pl.ds(j * NBLK, NBLK)
        hi[rows, :], lo[rows, :] = split(turned)
    copies[2].wait()
    copies[3].wait()
    g_hi, g_lo = split(second_ref[0])
    spec[...] = mm(hi[...], g_hi) + mm(lo[...], g_hi) + mm(hi[...], g_lo)
    for c in range(8):
        s = spec[pl.ds(2 * c * NBLK, NBLK), :]
        f = spec[pl.ds((2 * c + 1) * NBLK, NBLK), :]
        sr, si, fr, fi = s[:, :BLOCK], s[:, BLOCK:], f[:, :BLOCK], f[:, BLOCK:]
        rows = pl.ds(c * NBLK, NBLK)
        hi[rows, :], lo[rows, :] = split(jnp.concatenate([sr * fr - si * fi, sr * fi + si * fr], 1))
    half = pl.ds(0, 8 * NBLK)
    g_hi, g_lo = split(second_ref[1])
    spec[half, :] = mm(hi[half, :], g_hi) + mm(lo[half, :], g_hi) + mm(hi[half, :], g_lo)
    for c in range(8):
        b = spec[pl.ds(c * NBLK, NBLK), :]
        br, bi = b[:, :BLOCK], b[:, BLOCK:]
        d_hi, d_lo = split(jnp.concatenate([br * tre + bi * tim, bi * tre - br * tim], 0))
        at = pl.ds(c * BLOCK, BLOCK)
        dd[0:128, at] = d_hi
        dd[128:256, at] = d_lo
        dd[256:384, at] = d_hi
    l_hi, l_lo = split(last_ref[...])
    y = mm(jnp.concatenate([l_hi, l_hi, l_lo], 1), dd[...])
    at = lax.axis_index("z")
    own = 64 * (at // 2) + 16 * lax.axis_index("x") + 8 * (at % 2)
    for c in range(8):
        direct = skip_ref[own + c] * xs[:, c, :]
        ys[:, c, :] = y[:, c * BLOCK : (c + 1) * BLOCK] + direct
    for x in range(4):
        out_ref[:, x] = ys[pl.ds(16 * x, 16)].astype(BF16)


def gate_kernel(r_ref, side_ref, out_ref):
    for x in range(4):
        conv = r_ref[:, x].astype(F32).reshape(BLOCK, BLOCK)
        out_ref[x] = (conv * side_ref[x, 0:BLOCK].astype(F32)).T.astype(BF16)


def project_kernel(mine_ref, other_ref, w_ref, out_ref):
    core = lax.axis_index("core")
    left, right = [], []
    for side, ref in enumerate((mine_ref, other_ref)):
        group = pl.ds(8 * (core if side == 0 else 1 - core), 8)
        for y in range(4):
            left.append(ref[y].reshape(4 * BLOCK, BLOCK))
            w = w_ref[group, y, SPARE:].reshape(8, 4, 16, BLOCK)
            right.append(jnp.concatenate([w[:, q].reshape(BLOCK, BLOCK) for q in range(4)], 1))
    total = mm(jnp.concatenate(left, 1), jnp.concatenate(right, 0))
    out_ref[...] = total.astype(BF16).reshape(4, BLOCK, 512)


def sum_kernel(p_ref, out_ref):
    p = p_ref[...].astype(F32)
    out_ref[...] = ((p[0] + p[1]) + (p[2] + p[3])).astype(BF16)


PARAMS = pltpu.CompilerParams(vmem_limit_bytes=VMEM_LIMIT)


def shape(dims, kind=BF16):
    return jax.ShapeDtypeStruct(dims, kind)


ANY = pl.BlockSpec(memory_space=pl.ANY)
SCALARS = pl.BlockSpec(memory_space=pltpu.SMEM)
INSIDE = pl.BlockSpec(memory_space=pltpu.VMEM)


def call(body, out, ins, scratch):
    return pl.pallas_call(
        body, out_shape=shape(out), in_specs=ins, out_specs=INSIDE, scratch_shapes=scratch, compiler_params=PARAMS
    )


def copies(count):
    return pltpu.SemaphoreType.DMA((count,))


def run_conv(moved, skip):
    first, twist, second, last = tables()
    return call(
        conv_kernel,
        (16, 4, 8, BLOCK),
        [INSIDE, SCALARS, ANY, ANY, ANY, ANY],
        [
            pltpu.VMEM((NBLK, 16, BLOCK), F32),
            pltpu.VMEM((128, 16 * BLOCK), BF16),
            pltpu.VMEM((16 * NBLK, 256), BF16),
            pltpu.VMEM((16 * NBLK, 256), BF16),
            pltpu.VMEM((16 * NBLK, 256), F32),
            pltpu.VMEM((384, 8 * BLOCK), BF16),
            pltpu.VMEM((NBLK, 8, BLOCK), F32),
            pltpu.VMEM(first.shape, F32),
            pltpu.VMEM(twist.shape, F32),
            pltpu.VMEM(second.shape, F32),
            pltpu.VMEM(last.shape, F32),
            copies(4),
        ],
    )(moved, skip, first, twist, second, last)


def per_device(gate_in, value_in, gate_out, filters, skip_gain, out_weight):
    tile = pltpu.VMEM((BLOCK, 512), BF16)
    packed, side = pl.pallas_call(
        pack_kernel,
        out_shape=(shape((NBLK, 16, BLOCK)), shape((4, 192, BLOCK))),
        in_specs=[ANY] * 5,
        out_specs=(INSIDE, INSIDE),
        scratch_shapes=[tile] * 4 + [pltpu.VMEM((64, 512), BF16), copies(5)],
        compiler_params=pltpu.CompilerParams(vmem_limit_bytes=60 * 1024 * 1024),
    )(gate_in, value_in, filters, gate_out, out_weight)
    side = lax.all_to_all(side, "x", split_axis=0, concat_axis=0, tiled=True)
    packed, side = lax.optimization_barrier((packed, side))
    weight = lax.all_gather(side[:, BLOCK - SPARE :], "z", axis=0)
    moved = lax.all_to_all(packed, ("x", "z"), split_axis=0, concat_axis=0, tiled=True)
    conv = run_conv(moved, skip_gain)
    back = lax.all_to_all(conv, "z", split_axis=0, concat_axis=0, tiled=True)
    gated = call(gate_kernel, (4, BLOCK, BLOCK), [INSIDE, INSIDE], [])(back, side)
    mine = lax.all_to_all(
        jnp.broadcast_to(gated[None], (4, 4, BLOCK, BLOCK)), "y", split_axis=0, concat_axis=0, tiled=True
    )
    other = lax.ppermute(mine, "core", [(0, 1), (1, 0)])
    partial = call(
        project_kernel,
        (4, BLOCK, 512),
        [INSIDE, INSIDE, INSIDE],
        [],
    )(mine, other, weight)
    parts = lax.all_to_all(partial, "x", split_axis=0, concat_axis=0, tiled=True)
    return call(sum_kernel, (BLOCK, 512), [INSIDE], [])(parts)


def solution(mesh):
    fine = Mesh(mesh.devices.reshape(4, 16, 4, 2), ("x", "z", "y", "core"))
    rows, cols = ("x", "z"), ("y", "core")
    whole = P(rows, cols)
    return jax.shard_map(
        per_device,
        mesh=fine,
        in_specs=(whole, whole, whole, whole, P(cols), whole),
        out_specs=whole,
        check_vma=False,
    )
```

```python
import math

import jax
import jax.numpy as jnp
import numpy as np
from jax import lax
from jax.experimental import pallas as pl
from jax.experimental.pallas import tpu as pltpu
from jax.sharding import Mesh
from jax.sharding import PartitionSpec as P

F32 = jnp.float32
BF16 = jnp.bfloat16
SEQ = 8192
BLOCK = 128
NBLK = SEQ // BLOCK
SPARE = 16
VMEM_LIMIT = 24 * 1024 * 1024


def tables():
    n1 = np.arange(NBLK)
    k1 = np.arange(NBLK) + 0.25
    n2 = np.arange(BLOCK)
    ang = 2.0 * math.pi / NBLK * (k1[:, None] * n1[None, :])
    first = np.concatenate([np.cos(ang), -np.sin(ang)], 0)
    first = np.concatenate([first, first], 1).astype(np.float32)
    tw = 2.0 * math.pi / SEQ * (k1[:, None] * n2[None, :])
    twist = np.stack([np.cos(tw), -np.sin(tw)]).astype(np.float32)
    th = 2.0 * math.pi / BLOCK * ((n2[:, None] * n2[None, :]) % BLOCK)
    c, s = np.cos(th), np.sin(th)
    fwd = np.block([[c, -s], [s, c]])
    second = np.stack([fwd, fwd.T]).astype(np.float32)
    last = (np.concatenate([np.cos(ang.T), -np.sin(ang.T)], 1) / SEQ).astype(np.float32)
    return first, twist, second, last


def split(x):
    high = x.astype(BF16)
    return high, (x - high.astype(F32)).astype(BF16)


def mm(a, b):
    return jnp.dot(a, b, preferred_element_type=F32)


def fetch(sources, buffers, sems):
    copies = [pltpu.make_async_copy(s, b, sems.at[i]) for i, (s, b) in enumerate(zip(sources, buffers))]
    for copy in copies:
        copy.start()
    return copies


def by_owner(x):
    x = x.reshape(8, 4, 16, BLOCK)
    return jnp.stack([x[:, owner] for owner in range(4)])


def pack_kernel(gi_hbm, vi_hbm, f_hbm, go_hbm, w_hbm, out_ref, side_ref, gi_ref, vi_ref, f_ref, go_ref, w_ref, sems):
    loads = fetch((go_hbm, w_hbm, gi_hbm, vi_hbm, f_hbm), (go_ref, w_ref, gi_ref, vi_ref, f_ref), sems)
    for load in loads:
        load.wait()
    gate = by_owner(go_ref[...].astype(F32).T).reshape(4, BLOCK, BLOCK)
    w = w_ref[...].astype(F32).reshape(4, 16, 512)
    rows = [w[:, :, q * BLOCK : (q + 1) * BLOCK] for q in range(4)]
    side_ref[...] = jnp.concatenate([gate] + rows, 1).astype(BF16)
    signal = (gi_ref[...].astype(F32) * vi_ref[...].astype(F32)).astype(BF16)
    sig_t = by_owner(signal.astype(F32).T).reshape(NBLK, 8, BLOCK)
    fil_t = by_owner(f_ref[...].astype(F32).T).reshape(NBLK, 8, BLOCK)
    out_ref[...] = jnp.concatenate([sig_t, fil_t], 1).astype(BF16)


def conv_kernel(
    r_ref, skip_ref, first_ref, twist_ref, second_ref, last_ref, out_ref, xs, xx, hi, lo, spec, dd, ys
):
    xs[...] = r_ref[...].astype(F32)
    for c in range(8):
        for part in range(2):
            x = xs[:, 8 * part + c, :].astype(BF16)
            at = pl.ds((2 * c + part) * BLOCK, BLOCK)
            xx[0:NBLK, at] = x
            xx[NBLK:, at] = x
    tre, tim = twist_ref[0], twist_ref[1]
    f_hi, f_lo = split(first_ref[...])
    lanes = lax.broadcasted_iota(jnp.int32, f_hi.shape, 1)
    first = jnp.where(lanes < NBLK, f_hi.astype(F32), f_lo.astype(F32)).astype(BF16)
    for j in range(16):
        a = mm(first, xx[:, j * BLOCK : (j + 1) * BLOCK])
        re, im = a[:NBLK], a[NBLK:]
        turned = jnp.concatenate([re * tre - im * tim, re * tim + im * tre], 1)
        rows = pl.ds(j * NBLK, NBLK)
        hi[rows, :], lo[rows, :] = split(turned)
    g_hi, g_lo = split(second_ref[0])
    spec[...] = mm(hi[...], g_hi) + mm(lo[...], g_hi) + mm(hi[...], g_lo)
    for c in range(8):
        s = spec[pl.ds(2 * c * NBLK, NBLK), :]
        f = spec[pl.ds((2 * c + 1) * NBLK, NBLK), :]
        sr, si, fr, fi = s[:, :BLOCK], s[:, BLOCK:], f[:, :BLOCK], f[:, BLOCK:]
        rows = pl.ds(c * NBLK, NBLK)
        hi[rows, :], lo[rows, :] = split(jnp.concatenate([sr * fr - si * fi, sr * fi + si * fr], 1))
    half = pl.ds(0, 8 * NBLK)
    g_hi, g_lo = split(second_ref[1])
    spec[half, :] = mm(hi[half, :], g_hi) + mm(lo[half, :], g_hi) + mm(hi[half, :], g_lo)
    for c in range(8):
        b = spec[pl.ds(c * NBLK, NBLK), :]
        br, bi = b[:, :BLOCK], b[:, BLOCK:]
        d_hi, d_lo = split(jnp.concatenate([br * tre + bi * tim, bi * tre - br * tim], 0))
        at = pl.ds(c * BLOCK, BLOCK)
        dd[0:128, at] = d_hi
        dd[128:256, at] = d_lo
        dd[256:384, at] = d_hi
    l_hi, l_lo = split(last_ref[...])
    y = mm(jnp.concatenate([l_hi, l_hi, l_lo], 1), dd[...])
    at = lax.axis_index("z")
    own = 64 * (at // 2) + 16 * lax.axis_index("x") + 8 * (at % 2)
    for c in range(8):
        direct = skip_ref[own + c] * xs[:, c, :]
        ys[:, c, :] = y[:, c * BLOCK : (c + 1) * BLOCK] + direct
    for x in range(4):
        out_ref[:, x] = ys[pl.ds(16 * x, 16)].astype(BF16)


def gate_kernel(r_ref, side_ref, out_ref):
    for x in range(4):
        conv = r_ref[:, x].astype(F32).reshape(BLOCK, BLOCK)
        out_ref[x] = (conv * side_ref[x, 0:BLOCK].astype(F32)).T.astype(BF16)


def project_kernel(mine_ref, other_ref, w_ref, out_ref):
    core = lax.axis_index("core")
    left, right = [], []
    for side, ref in enumerate((mine_ref, other_ref)):
        group = pl.ds(8 * (core if side == 0 else 1 - core), 8)
        for y in range(4):
            left.append(ref[y].reshape(4 * BLOCK, BLOCK))
            w = w_ref[group, y, SPARE:].reshape(8, 4, 16, BLOCK)
            right.append(jnp.concatenate([w[:, q].reshape(BLOCK, BLOCK) for q in range(4)], 1))
    total = mm(jnp.concatenate(left, 1), jnp.concatenate(right, 0))
    out_ref[...] = total.astype(BF16).reshape(4, BLOCK, 512)


def sum_kernel(p_ref, out_ref):
    p = p_ref[...].astype(F32)
    out_ref[...] = ((p[0] + p[1]) + (p[2] + p[3])).astype(BF16)


PARAMS = pltpu.CompilerParams(vmem_limit_bytes=VMEM_LIMIT)


def shape(dims, kind=BF16):
    return jax.ShapeDtypeStruct(dims, kind)


ANY = pl.BlockSpec(memory_space=pl.ANY)
SCALARS = pl.BlockSpec(memory_space=pltpu.SMEM)
INSIDE = pl.BlockSpec(memory_space=pltpu.VMEM)


def call(body, out, ins, scratch):
    return pl.pallas_call(
        body, out_shape=shape(out), in_specs=ins, out_specs=INSIDE, scratch_shapes=scratch, compiler_params=PARAMS
    )


def copies(count):
    return pltpu.SemaphoreType.DMA((count,))


def run_conv(moved, skip):
    first, twist, second, last = tables()
    return call(
        conv_kernel,
        (16, 4, 8, BLOCK),
        [INSIDE, SCALARS, INSIDE, INSIDE, INSIDE, INSIDE],
        [
            pltpu.VMEM((NBLK, 16, BLOCK), F32),
            pltpu.VMEM((128, 16 * BLOCK), BF16),
            pltpu.VMEM((16 * NBLK, 256), BF16),
            pltpu.VMEM((16 * NBLK, 256), BF16),
            pltpu.VMEM((16 * NBLK, 256), F32),
            pltpu.VMEM((384, 8 * BLOCK), BF16),
            pltpu.VMEM((NBLK, 8, BLOCK), F32),
        ],
    )(moved, skip, first, twist, second, last)


def per_device(gate_in, value_in, gate_out, filters, skip_gain, out_weight):
    tile = pltpu.VMEM((BLOCK, 512), BF16)
    packed, side = pl.pallas_call(
        pack_kernel,
        out_shape=(shape((NBLK, 16, BLOCK)), shape((4, 192, BLOCK))),
        in_specs=[ANY] * 5,
        out_specs=(INSIDE, INSIDE),
        scratch_shapes=[tile] * 4 + [pltpu.VMEM((64, 512), BF16), copies(5)],
        compiler_params=pltpu.CompilerParams(vmem_limit_bytes=60 * 1024 * 1024),
    )(gate_in, value_in, filters, gate_out, out_weight)
    side = lax.all_to_all(side, "x", split_axis=0, concat_axis=0, tiled=True)
    packed, side = lax.optimization_barrier((packed, side))
    weight = lax.all_gather(side[:, BLOCK - SPARE :], "z", axis=0)
    moved = lax.all_to_all(packed, ("x", "z"), split_axis=0, concat_axis=0, tiled=True)
    conv = run_conv(moved, skip_gain)
    back = lax.all_to_all(conv, "z", split_axis=0, concat_axis=0, tiled=True)
    gated = call(gate_kernel, (4, BLOCK, BLOCK), [INSIDE, INSIDE], [])(back, side)
    mine = lax.all_to_all(
        jnp.broadcast_to(gated[None], (4, 4, BLOCK, BLOCK)), "y", split_axis=0, concat_axis=0, tiled=True
    )
    other = lax.ppermute(mine, "core", [(0, 1), (1, 0)])
    partial = call(
        project_kernel,
        (4, BLOCK, 512),
        [INSIDE, INSIDE, INSIDE],
        [],
    )(mine, other, weight)
    parts = lax.all_to_all(partial, "x", split_axis=0, concat_axis=0, tiled=True)
    return call(sum_kernel, (BLOCK, 512), [INSIDE], [])(parts)


def solution(mesh):
    fine = Mesh(mesh.devices.reshape(4, 16, 4, 2), ("x", "z", "y", "core"))
    rows, cols = ("x", "z"), ("y", "core")
    whole = P(rows, cols)
    return jax.shard_map(
        per_device,
        mesh=fine,
        in_specs=(whole, whole, whole, whole, P(cols), whole),
        out_specs=whole,
        check_vma=False,
    )
```

```python
import math

import jax
import jax.numpy as jnp
import numpy as np
from jax import lax
from jax.experimental import pallas as pl
from jax.experimental.pallas import tpu as pltpu
from jax.sharding import Mesh
from jax.sharding import PartitionSpec as P

F32 = jnp.float32
BF16 = jnp.bfloat16
SEQ = 8192
BLOCK = 128
NBLK = SEQ // BLOCK
SPARE = 16
VMEM_LIMIT = 24 * 1024 * 1024


def tables():
    n1 = np.arange(NBLK)
    k1 = np.arange(NBLK) + 0.25
    n2 = np.arange(BLOCK)
    ang = 2.0 * math.pi / NBLK * (k1[:, None] * n1[None, :])
    first = np.concatenate([np.cos(ang), -np.sin(ang)], 0)
    first = np.concatenate([first, first], 1).astype(np.float32)
    tw = 2.0 * math.pi / SEQ * (k1[:, None] * n2[None, :])
    twist = np.stack([np.cos(tw), -np.sin(tw)]).astype(np.float32)
    th = 2.0 * math.pi / BLOCK * ((n2[:, None] * n2[None, :]) % BLOCK)
    c, s = np.cos(th), np.sin(th)
    fwd = np.block([[c, -s], [s, c]])
    second = np.stack([fwd, fwd.T]).astype(np.float32)
    last = (np.concatenate([np.cos(ang.T), -np.sin(ang.T)], 1) / SEQ).astype(np.float32)
    return first, twist, second, last


def split(x):
    high = x.astype(BF16)
    return high, (x - high.astype(F32)).astype(BF16)


def mm(a, b):
    return jnp.dot(a, b, preferred_element_type=F32)


def fetch(sources, buffers, sems):
    copies = [pltpu.make_async_copy(s, b, sems.at[i]) for i, (s, b) in enumerate(zip(sources, buffers))]
    for copy in copies:
        copy.start()
    return copies


def by_owner(x):
    x = x.reshape(8, 4, 16, BLOCK)
    return jnp.stack([x[:, owner] for owner in range(4)])


def side_kernel(go_hbm, w_hbm, side_ref, go_ref, w_ref, sems):
    loads = fetch((go_hbm, w_hbm), (go_ref, w_ref), sems)
    for load in loads:
        load.wait()
    gate = by_owner(go_ref[...].astype(F32).T).reshape(4, BLOCK, BLOCK)
    w = w_ref[...].astype(F32).reshape(4, 16, 512)
    rows = [w[:, :, q * BLOCK : (q + 1) * BLOCK] for q in range(4)]
    side_ref[...] = jnp.concatenate([gate] + rows, 1).astype(BF16)


def pack_kernel(gi_hbm, vi_hbm, f_hbm, out_ref, gi_ref, vi_ref, f_ref, sems):
    for load in fetch((gi_hbm, vi_hbm, f_hbm), (gi_ref, vi_ref, f_ref), sems):
        load.wait()
    signal = (gi_ref[...].astype(F32) * vi_ref[...].astype(F32)).astype(BF16)
    sig_t = by_owner(signal.astype(F32).T).reshape(NBLK, 8, BLOCK)
    fil_t = by_owner(f_ref[...].astype(F32).T).reshape(NBLK, 8, BLOCK)
    out_ref[...] = jnp.concatenate([sig_t, fil_t], 1).astype(BF16)


def conv_kernel(
    r_ref, skip_ref, first_ref, twist_ref, second_ref, last_ref, out_ref, xs, xx, hi, lo, spec, dd, ys
):
    xs[...] = r_ref[...].astype(F32)
    for c in range(8):
        for part in range(2):
            x = xs[:, 8 * part + c, :].astype(BF16)
            at = pl.ds((2 * c + part) * BLOCK, BLOCK)
            xx[0:NBLK, at] = x
            xx[NBLK:, at] = x
    tre, tim = twist_ref[0], twist_ref[1]
    f_hi, f_lo = split(first_ref[...])
    lanes = lax.broadcasted_iota(jnp.int32, f_hi.shape, 1)
    first = jnp.where(lanes < NBLK, f_hi.astype(F32), f_lo.astype(F32)).astype(BF16)
    for j in range(16):
        a = mm(first, xx[:, j * BLOCK : (j + 1) * BLOCK])
        re, im = a[:NBLK], a[NBLK:]
        turned = jnp.concatenate([re * tre - im * tim, re * tim + im * tre], 1)
        rows = pl.ds(j * NBLK, NBLK)
        hi[rows, :], lo[rows, :] = split(turned)
    g_hi, g_lo = split(second_ref[0])
    spec[...] = mm(hi[...], g_hi) + mm(lo[...], g_hi) + mm(hi[...], g_lo)
    for c in range(8):
        s = spec[pl.ds(2 * c * NBLK, NBLK), :]
        f = spec[pl.ds((2 * c + 1) * NBLK, NBLK), :]
        sr, si, fr, fi = s[:, :BLOCK], s[:, BLOCK:], f[:, :BLOCK], f[:, BLOCK:]
        rows = pl.ds(c * NBLK, NBLK)
        hi[rows, :], lo[rows, :] = split(jnp.concatenate([sr * fr - si * fi, sr * fi + si * fr], 1))
    half = pl.ds(0, 8 * NBLK)
    g_hi, g_lo = split(second_ref[1])
    spec[half, :] = mm(hi[half, :], g_hi) + mm(lo[half, :], g_hi) + mm(hi[half, :], g_lo)
    for c in range(8):
        b = spec[pl.ds(c * NBLK, NBLK), :]
        br, bi = b[:, :BLOCK], b[:, BLOCK:]
        d_hi, d_lo = split(jnp.concatenate([br * tre + bi * tim, bi * tre - br * tim], 0))
        at = pl.ds(c * BLOCK, BLOCK)
        dd[0:128, at] = d_hi
        dd[128:256, at] = d_lo
        dd[256:384, at] = d_hi
    l_hi, l_lo = split(last_ref[...])
    y = mm(jnp.concatenate([l_hi, l_hi, l_lo], 1), dd[...])
    at = lax.axis_index("z")
    own = 64 * (at // 2) + 16 * lax.axis_index("x") + 8 * (at % 2)
    for c in range(8):
        direct = skip_ref[own + c] * xs[:, c, :]
        ys[:, c, :] = y[:, c * BLOCK : (c + 1) * BLOCK] + direct
    for x in range(4):
        out_ref[:, x] = ys[pl.ds(16 * x, 16)].astype(BF16)


def gate_kernel(r_ref, side_ref, out_ref):
    for x in range(4):
        conv = r_ref[:, x].astype(F32).reshape(BLOCK, BLOCK)
        out_ref[x] = (conv * side_ref[x, 0:BLOCK].astype(F32)).T.astype(BF16)


def project_kernel(mine_ref, other_ref, w_ref, out_ref):
    core = lax.axis_index("core")
    left, right = [], []
    for side, ref in enumerate((mine_ref, other_ref)):
        group = pl.ds(8 * (core if side == 0 else 1 - core), 8)
        for y in range(4):
            left.append(ref[y].reshape(4 * BLOCK, BLOCK))
            w = w_ref[group, y, SPARE:].reshape(8, 4, 16, BLOCK)
            right.append(jnp.concatenate([w[:, q].reshape(BLOCK, BLOCK) for q in range(4)], 1))
    total = mm(jnp.concatenate(left, 1), jnp.concatenate(right, 0))
    out_ref[...] = total.astype(BF16).reshape(4, BLOCK, 512)


def sum_kernel(p_ref, out_ref):
    p = p_ref[...].astype(F32)
    out_ref[...] = ((p[0] + p[1]) + (p[2] + p[3])).astype(BF16)


PARAMS = pltpu.CompilerParams(vmem_limit_bytes=VMEM_LIMIT)


def shape(dims, kind=BF16):
    return jax.ShapeDtypeStruct(dims, kind)


ANY = pl.BlockSpec(memory_space=pl.ANY)
SCALARS = pl.BlockSpec(memory_space=pltpu.SMEM)
INSIDE = pl.BlockSpec(memory_space=pltpu.VMEM)


def call(body, out, ins, scratch):
    return pl.pallas_call(
        body, out_shape=shape(out), in_specs=ins, out_specs=INSIDE, scratch_shapes=scratch, compiler_params=PARAMS
    )


def copies(count):
    return pltpu.SemaphoreType.DMA((count,))


def run_conv(moved, skip):
    first, twist, second, last = tables()
    return call(
        conv_kernel,
        (16, 4, 8, BLOCK),
        [INSIDE, SCALARS, INSIDE, INSIDE, INSIDE, INSIDE],
        [
            pltpu.VMEM((NBLK, 16, BLOCK), F32),
            pltpu.VMEM((128, 16 * BLOCK), BF16),
            pltpu.VMEM((16 * NBLK, 256), BF16),
            pltpu.VMEM((16 * NBLK, 256), BF16),
            pltpu.VMEM((16 * NBLK, 256), F32),
            pltpu.VMEM((384, 8 * BLOCK), BF16),
            pltpu.VMEM((NBLK, 8, BLOCK), F32),
        ],
    )(moved, skip, first, twist, second, last)


def per_device(gate_in, value_in, gate_out, filters, skip_gain, out_weight):
    tile = pltpu.VMEM((BLOCK, 512), BF16)
    wide = pltpu.CompilerParams(vmem_limit_bytes=60 * 1024 * 1024)
    side = pl.pallas_call(
        side_kernel,
        out_shape=shape((4, 192, BLOCK)),
        in_specs=[ANY] * 2,
        out_specs=INSIDE,
        scratch_shapes=[tile, pltpu.VMEM((64, 512), BF16), copies(2)],
        compiler_params=wide,
    )(gate_out, out_weight)
    side = lax.all_to_all(side, "x", split_axis=0, concat_axis=0, tiled=True)
    side, filters = lax.optimization_barrier((side, filters))
    packed = pl.pallas_call(
        pack_kernel,
        out_shape=shape((NBLK, 16, BLOCK)),
        in_specs=[ANY] * 3,
        out_specs=INSIDE,
        scratch_shapes=[tile] * 3 + [copies(3)],
        compiler_params=wide,
    )(gate_in, value_in, filters)
    weight = lax.all_gather(side[:, BLOCK - SPARE :], "z", axis=0)
    moved = lax.all_to_all(packed, ("x", "z"), split_axis=0, concat_axis=0, tiled=True)
    conv = run_conv(moved, skip_gain)
    back = lax.all_to_all(conv, "z", split_axis=0, concat_axis=0, tiled=True)
    gated = call(gate_kernel, (4, BLOCK, BLOCK), [INSIDE, INSIDE], [])(back, side)
    mine = lax.all_to_all(
        jnp.broadcast_to(gated[None], (4, 4, BLOCK, BLOCK)), "y", split_axis=0, concat_axis=0, tiled=True
    )
    other = lax.ppermute(mine, "core", [(0, 1), (1, 0)])
    partial = call(
        project_kernel,
        (4, BLOCK, 512),
        [INSIDE, INSIDE, INSIDE],
        [],
    )(mine, other, weight)
    parts = lax.all_to_all(partial, "x", split_axis=0, concat_axis=0, tiled=True)
    return call(sum_kernel, (BLOCK, 512), [INSIDE], [])(parts)


def solution(mesh):
    fine = Mesh(mesh.devices.reshape(4, 16, 4, 2), ("x", "z", "y", "core"))
    rows, cols = ("x", "z"), ("y", "core")
    whole = P(rows, cols)
    return jax.shard_map(
        per_device,
        mesh=fine,
        in_specs=(whole, whole, whole, whole, P(cols), whole),
        out_specs=whole,
        check_vma=False,
    )
```
